512 devices in a mesh: seq: 64 (over x, y, core), group: 8 (over z).
Axes of the slice: x: 4, y: 8, z: 8, core: 2. Of those that a mesh axis runs over, the one named last changes fastest.
Arguments:
- queries: bfloat16 [8, 16384, 4096], P('group', 'seq'), may hold values from -4.75 to 4.75
- keys_values: bfloat16 [8, 16384, 1024], P('group', 'seq'), may hold values from -4.75 to 4.75
- block_list: int32 [8, 128, 8], P('group', 'seq'), may hold values from 0 to 127, as said below
- value_dir: bfloat16 [4096], replicated, may hold values from -2 to 2
- base_values: float32 [8, 16384], P('group', 'seq'), may hold values from -6 to 6
- rewards: float32 [8, 16384], P('group', 'seq'), may hold values from -0.4375 to 0.4375
- turn_start: int32 [8, 16384], P('group', 'seq'), may hold values 0 or 1
- actor_shard: int32 [8, 16384], P('group', 'seq'), may hold values from 0 to 511, as said below
Outputs:
- token_values: float32 [8, 16384], P('group', 'seq')
- actor_advantages: float32 [131072], P(('seq', 'group'))
- actor_returns: float32 [131072], P(('seq', 'group'))
The draws below stay inside these ranges and needn't reach their ends.
Inputs may be any that keep to these rules, and one draw needn't show every extreme that they name: `block_list`: entry j of block b's list is a block of [max(0, b - 14), b]; an entry equal to b lists nothing. `actor_shard`: each sequence shard sends 256 // 8 of its positions to each group index of the actor's shards; of the positions held by the 8 shards of one seq index that go to one group index, exactly 4 go to each seq index. The actor's shard d has seq index d // 8 and group index d % 8.
All inputs are finite; a program needn't handle non-finite values. No bound on the sum of `turn_start` on one device may be relied on, other than what follows from the above.
Results may differ from the reference program's by a relative error of at most 0.0049.
Values may be sent and summed in bfloat16 or wider, within the bound.
No kernel may reach another device: no remote copies, remote signals or barrier semaphores. Data moves between devices by JAX's collectives and lax.ppermute only.
A program may use at most 64 MiB of HBM per device.

```python
import jax
import jax.numpy as jnp
from jax import lax

H = 32
KVH = 4
HD = 128
BLK = 128
WIN = 7
LIST = 8
TOK_DEV = 256
QB = 2
GROUPS = 8
SHARDS = 64
TOKENS = 16384
NBLK = 128


def draw_queries(key, part):
    key = jax.random.fold_in(key, 5)
    shape = (GROUPS, TOKENS, H * HD)
    result = jax.random.truncated_normal(key, -4.75, 4.75, shape, jnp.float32)
    return jnp.clip(result, -4.75, 4.75).astype(jnp.bfloat16)


def draw_keys_values(key, part):
    key = jax.random.fold_in(key, 6)
    shape = (GROUPS, TOKENS, 2 * KVH * HD)
    result = jax.random.truncated_normal(key, -4.75, 4.75, shape, jnp.float32)
    return jnp.clip(result, -4.75, 4.75).astype(jnp.bfloat16)


def draw_block_list(key, part):
    key = jax.random.fold_in(key, 7)
    breadth = jax.random.randint(key, (GROUPS, NBLK, 1), 0, LIST + 1)
    offset = jax.random.randint(jax.random.fold_in(key, 1), (GROUPS, NBLK, LIST), 1, WIN * QB + 1)
    block = jnp.arange(NBLK, dtype=jnp.int32)[None, :, None]
    listed = block - offset
    used = (jnp.arange(LIST)[None, None, :] < breadth) & (listed >= 0)
    return jnp.where(used, listed, block).astype(jnp.int32)


def draw_actor_shard(key, part):
    key = jax.random.fold_in(key, 9)
    per_group = TOK_DEV // GROUPS
    per_shard = TOK_DEV // SHARDS
    first_scores = jax.random.randint(key, (GROUPS, SHARDS, TOK_DEV), 0, 1 << 20) * TOK_DEV + jnp.arange(TOK_DEV)
    dest_group = jnp.argsort(first_scores, axis=-1).astype(jnp.int32) // per_group
    onehot = (dest_group[..., None] == jnp.arange(GROUPS)).astype(jnp.int32)
    rank = jnp.sum(onehot * (jnp.cumsum(onehot, axis=2) - 1), axis=-1)
    source = jnp.arange(GROUPS, dtype=jnp.int32)[:, None, None]
    slot = source * per_group + rank
    second_scores = jax.random.randint(jax.random.fold_in(key, 1), (SHARDS, GROUPS, TOK_DEV), 0, 1 << 20) * TOK_DEV + jnp.arange(TOK_DEV)
    mixing = jnp.argsort(second_scores, axis=-1).astype(jnp.int32)
    shard_index = jnp.arange(SHARDS, dtype=jnp.int32)[None, :, None]
    flat = (shard_index * GROUPS + dest_group) * TOK_DEV + slot
    dest_shard = mixing.reshape(-1)[flat] // per_shard
    return (dest_shard * GROUPS + dest_group).reshape(GROUPS, SHARDS * TOK_DEV).astype(jnp.int32)


def set_ends(values, stream_key, least, largest):
    spot = [jax.random.randint(jax.random.fold_in(stream_key, axis), (), 0, length) for axis, length in enumerate(values.shape)]
    widest = values.shape.index(max(values.shape))
    neighbour = spot[:widest] + [(spot[widest] + 1) % values.shape[widest]] + spot[widest + 1:]
    return values.at[tuple(spot)].set(least).at[tuple(neighbour)].set(largest)


def block_levels(key, extent, pieces, smallest, largest):
    gain = 1.0
    for dim, shards_of in pieces:
        draws = jax.random.uniform(jax.random.fold_in(jax.random.fold_in(key, 6), dim), (shards_of,), jnp.float32, smallest / len(pieces), largest / len(pieces))
        gain = gain * jnp.repeat(jnp.exp(draws), extent[dim] // shards_of).reshape((-1,) + (1,) * (len(extent) - 1 - dim))
    return gain


def gaussian(key, dims, spread, bound, pieces=(), kind=jnp.bfloat16):
    factor_of = block_levels(key, dims, pieces, -0.22, 0.18) if pieces else 1.0
    array = jax.random.normal(key, dims, jnp.float32) * spread * factor_of
    return jnp.minimum(jnp.maximum(array, -bound), bound).astype(kind)


def setup_inputs(seed: int = 0) -> dict:
    streams_of = jax.random.split(jax.random.key(seed), 9)
    queries = draw_queries(jax.random.fold_in(streams_of[8], 71), 0)
    keys_values = draw_keys_values(jax.random.fold_in(streams_of[8], 71), 0)
    block_list = draw_block_list(jax.random.fold_in(streams_of[8], 71), 0)
    value_dir = gaussian(streams_of[3], (H * HD,), 0.15, 2.0)
    base_values = gaussian(streams_of[4], (GROUPS, TOKENS), 1.0, 6.0, ((0, 8), (1, 64)), jnp.float32)
    rewards = gaussian(streams_of[5], (GROUPS, TOKENS), 0.03, 0.4375, ((0, 8), (1, 64)), jnp.float32)
    turn_start = set_ends((jax.random.randint(streams_of[6], (GROUPS, TOKENS), 0, 64) < 1).astype(jnp.int32), jax.random.fold_in(streams_of[6], 1), 0, 1)
    actor_shard = draw_actor_shard(jax.random.fold_in(streams_of[8], 71), 0)
    return dict(queries=queries, keys_values=keys_values, block_list=block_list, value_dir=value_dir, base_values=base_values, rewards=rewards, turn_start=turn_start, actor_shard=actor_shard)


TRACE = 0.995


def listed_mask(entries, block):
    earlier = entries < block
    same = entries[:, None] == entries[None, :]
    before = jnp.arange(LIST)[None, :] < jnp.arange(LIST)[:, None]
    repeat = jnp.any(same & before, axis=1)
    return earlier & jnp.logical_not(repeat)


def block_values(query_rows, blocks, entries, block, direction, base_rows):
    width = KVH * HD
    query_block = query_rows.astype(jnp.float32).reshape(BLK, KVH, H // KVH, HD)
    valid = listed_mask(entries, block)
    chosen = blocks[jnp.concatenate([block[None], entries]).astype(jnp.int32)]
    keys = chosen[:, :, :width].astype(jnp.float32).reshape(LIST + 1, BLK, KVH, HD)
    values = chosen[:, :, width:].astype(jnp.float32).reshape(LIST + 1, BLK, KVH, HD)
    scores = jnp.einsum("qkgd,nskd->kgqns", query_block, keys, precision=lax.Precision.HIGHEST) * (HD ** -0.5)
    diag = (jnp.arange(BLK)[None, :] <= jnp.arange(BLK)[:, None])[:, None, :]
    seen = jnp.concatenate([jnp.ones((1,), bool), valid])
    first = (jnp.arange(LIST + 1) == 0)[None, :, None]
    mask = jnp.where(first, diag, seen[None, :, None])
    scores = jnp.where(mask, scores, -1e30)
    peak = jnp.max(scores, axis=(3, 4), keepdims=True)
    expo = jnp.exp(scores - peak)
    shares = lax.optimization_barrier(expo.astype(jnp.bfloat16)).astype(jnp.float32)
    totals = jnp.sum(expo, axis=(3, 4))
    summed = jnp.einsum("kgqns,nskd->qkgd", shares, values, precision=lax.Precision.HIGHEST)
    attended = (summed / jnp.transpose(totals, (2, 0, 1))[..., None]).astype(jnp.bfloat16)
    attended = attended.reshape(BLK, H * HD)
    return jnp.dot(attended, direction, preferred_element_type=jnp.float32) + base_rows


def trajectory_values(item, direction):
    query_all, pairs, lists, base = item
    blocks = pairs.reshape(NBLK, BLK, 2 * KVH * HD)

    def one_block(block):
        rows = lax.dynamic_slice_in_dim(query_all, block * BLK, BLK, 0)
        base_rows = lax.dynamic_slice_in_dim(base, block * BLK, BLK, 0)
        return block_values(rows, blocks, lists[block], block, direction, base_rows)

    return lax.map(one_block, jnp.arange(NBLK, dtype=jnp.int32)).reshape(TOKENS)


def gae_chain(item):
    values, gains, starts = item

    def step(carry, entry):
        nxt_adv, nxt_val, pending = carry
        value, reward, start = entry
        advantage = pending + reward + nxt_val + TRACE * nxt_adv - value
        carry = (jnp.where(start, advantage, nxt_adv), jnp.where(start, value, nxt_val), jnp.where(start, 0.0 * pending, pending + reward))
        return carry, advantage

    zero = jnp.zeros((), jnp.float32)
    _, advantage = lax.scan(step, (zero, zero, zero), (values, gains, starts), reverse=True)
    return advantage


def actor_layout(field, order):
    flat = jnp.transpose(field.reshape(GROUPS, SHARDS, TOK_DEV), (1, 0, 2)).reshape(GROUPS * TOKENS)
    return flat[order]


def reference(queries, keys_values, block_list, value_dir, base_values, rewards, turn_start, actor_shard):
    token_values = lax.map(lambda item: trajectory_values(item, value_dir), (queries, keys_values, block_list, base_values))
    starts = (turn_start == 1) | (jnp.arange(TOKENS)[None, :] == 0)
    advantage = lax.map(gae_chain, (token_values, rewards, starts))
    returns = advantage + token_values
    dest = jnp.transpose(actor_shard.reshape(GROUPS, SHARDS, TOK_DEV), (1, 0, 2)).reshape(GROUPS * TOKENS)
    order = jnp.argsort(dest * (GROUPS * TOKENS) + jnp.arange(GROUPS * TOKENS, dtype=jnp.int32)).astype(jnp.int32)
    return token_values, actor_layout(advantage, order), actor_layout(returns, order)
```

```python
import math

import jax
import jax.numpy as jnp
from jax import lax
from jax.experimental import pallas as pl
from jax.experimental.pallas import tpu as pltpu
from jax.sharding import PartitionSpec as P

HD = 128
BLK = 128
TOK = 256
KVH = 4
HEADS = 32
PER = HEADS // KVH
HALF = KVH * HD
LIST = 8
MSG = TOK + HEADS // 2
TRACE = 0.995
LOG_TRACE = math.log(TRACE)
TO_LOG2 = HD ** -0.5 * math.log2(math.e)
LOW = -1e30
F32 = jnp.float32
BF16 = jnp.bfloat16

NT = (((1,), (1,)), ((), ()))
SMEM = pl.BlockSpec(memory_space=pltpu.SMEM)
VMEM = pl.BlockSpec(memory_space=pltpu.VMEM)


def iota(shape, dim):
    return lax.broadcasted_iota(jnp.int32, shape, dim)


def three(x):
    first = x.astype(BF16)
    rest = x - first.astype(F32)
    second = rest.astype(BF16)
    third = (rest - second.astype(F32)).astype(BF16)
    return first, second, third


def message_kernel(kv_ref, dir_ref, out_ref):
    out_ref[0:TOK, :] = kv_ref[:, 0:HALF]
    direction = dir_ref[...]
    head = iota((HEADS, HD), 0)
    zero = jnp.zeros_like(direction)
    spread = jnp.concatenate(
        [jnp.where(head // PER == k, direction, zero) for k in range(KVH)], axis=1
    )
    read = lax.dot_general(
        spread, kv_ref[:, HALF:], NT, preferred_element_type=F32
    ).astype(BF16)
    out_ref[TOK:MSG, 0:TOK] = read[0 : HEADS // 2]
    out_ref[TOK:MSG, TOK:HALF] = read[HEADS // 2 :]


def message(kv, direction):
    return pl.pallas_call(
        message_kernel,
        out_shape=jax.ShapeDtypeStruct((MSG, HALF), BF16),
        in_specs=[VMEM, VMEM],
        out_specs=VMEM,
        cost_estimate=pl.CostEstimate(
            flops=2 * TOK * HALF * HEADS, bytes_accessed=800_000, transcendentals=0
        ),
        name="message",
    )(kv, direction)


def weights_kernel(place_ref, rew_ref, turn_ref, base_ref, dest_ref, m_ref, oh_ref, row_ref, col_ref):
    shard = place_ref[0]
    sub, lane = iota((TOK, TOK), 0), iota((TOK, TOK), 1)
    diag = sub == lane

    def column(row):
        return jnp.sum(jnp.where(diag, row, 0.0), axis=1, keepdims=True)

    spot = iota((1, TOK), 1)
    begins = (turn_ref[...] == 1) | ((shard == 0) & (spot == 0))
    start_row = jnp.where(begins, 1.0, 0.0)
    start_col = column(start_row)
    c_row = jnp.sum(jnp.where(sub <= lane, start_col, 0.0), axis=0, keepdims=True)
    c_col = jnp.sum(jnp.where(lane <= sub, start_row, 0.0), axis=1, keepdims=True)
    rewards = column(rew_ref[...])
    base = column(base_ref[...])
    gap = c_col - c_row
    opens = start_col > 0.5
    m = jnp.where((sub > lane) & opens, (1.0 - TRACE) * jnp.exp((gap - 1.0) * LOG_TRACE), 0.0)
    m_ref[...] = m
    decay = jnp.where(sub >= lane, jnp.exp(gap * LOG_TRACE), 0.0)
    known = jnp.sum(decay * rewards + m * base, axis=0, keepdims=True)
    total = jnp.sum(start_row, axis=1, keepdims=True)
    b_col = jnp.where(opens, (1.0 - TRACE) * jnp.exp((c_col - 1.0) * LOG_TRACE), 0.0)
    col_ref[...] = jnp.broadcast_to(b_col, (TOK, HD))
    b_known = jnp.sum(b_col * base + jnp.exp(c_col * LOG_TRACE) * rewards, axis=0, keepdims=True)
    dest = dest_ref[...]
    to_group = lax.rem(dest, 8).astype(F32)
    to_seq = (dest // 8).astype(F32)
    group_col = column(to_group)
    rank = jnp.sum(jnp.where((group_col == to_group) & (lane < sub), 1.0, 0.0), axis=1, keepdims=True)
    slot = (group_col * 32.0 + rank).astype(jnp.int32)
    oh_ref[...] = jnp.where(slot == lane, 1.0, 0.0).astype(BF16)
    wide = (1, TOK)
    rows = [
        base_ref[...],
        known,
        jnp.exp((total - c_row) * LOG_TRACE),
        to_seq,
        jnp.broadcast_to(jnp.exp(total * LOG_TRACE), wide),
        jnp.broadcast_to(b_known, wide),
        jnp.zeros(wide, F32),
        jnp.zeros(wide, F32),
    ]
    row_ref[...] = jnp.concatenate(rows, axis=0)


def weights(place, rewards, turns, base, dest):
    return pl.pallas_call(
        weights_kernel,
        out_shape=(
            jax.ShapeDtypeStruct((TOK, TOK), F32),
            jax.ShapeDtypeStruct((TOK, TOK), BF16),
            jax.ShapeDtypeStruct((8, TOK), F32),
            jax.ShapeDtypeStruct((TOK, HD), F32),
        ),
        in_specs=[SMEM, VMEM, VMEM, VMEM, VMEM],
        out_specs=(VMEM, VMEM, VMEM, VMEM),
        cost_estimate=pl.CostEstimate(flops=2_000_000, bytes_accessed=600_000, transcendentals=200_000),
        name="weights",
    )(place, rewards, turns, base, dest)


def attend_kernel(slots, has_own, place_ref, list_ref, q_ref, *rest):
    count = len(slots)
    msgs, out_ref, keys, reads, scores, found = rest[:count], *rest[count:]
    shard = place_ref[0]
    core = lax.rem(shard, 2)
    for i, msg in enumerate(msgs):
        for half in range(2):
            keys[2 * i + half] = msg[half * BLK : (half + 1) * BLK, :]
            for part in range(2):
                at = part * TOK + half * BLK
                reads[2 * i + half, part * 16 : (part + 1) * 16, :] = msg[
                    TOK:MSG, at : at + BLK
                ].astype(F32)
    for qb in range(2):
        block = shard * 2 + qb
        n = jnp.int32(0)
        entries = [list_ref[qb, j] for j in range(LIST)]
        for j in range(LIST):
            found[qb, j] = 0
        for j in range(LIST):
            entry = entries[j]
            use = entry < block
            for i in range(j):
                use = use & (entries[i] != entry)
            back = shard - entry // 2
            even = lax.rem(back, 2) == 0
            slot = jnp.where(even, back // 2, 4 + lax.rem(back // 2 + 1 - core, 4))
            local = jnp.int32(0)
            here = jnp.bool_(False)
            for i, s in enumerate(slots):
                hit = slot == s
                local = jnp.where(hit, 2 * i, local)
                here = here | hit
            found[qb, jnp.minimum(n, LIST - 1)] = jnp.where(
                use & here, local + lax.rem(entry, 2), found[qb, jnp.minimum(n, LIST - 1)]
            )
            n = n + jnp.where(use & here, 1, 0)
        found[qb, LIST] = n

    lane = iota((BLK, BLK), 1)
    causal = lane <= iota((BLK, BLK), 0)
    out_ref[...] = jnp.zeros_like(out_ref)

    def step(index, carry):
        qb, k = index // KVH, lax.rem(index, KVH)
        rows = pl.ds(pl.multiple_of(qb * BLK, BLK), BLK)
        n = found[qb, LIST]
        head_keys = pl.ds(pl.multiple_of(k * HD, HD), HD)

        def run(pairs):
            heads = [
                q_ref[rows, pl.ds(pl.multiple_of(k * (PER * HD) + g * HD, HD), HD)] for g in range(PER)
            ]
            query = jnp.concatenate(heads, axis=0)
            columns = []
            if has_own:
                own = qb + 2 * slots.index(0)
                columns.append(own)
                scores[:, 0:BLK] = lax.dot_general(
                    query, keys[own, :, head_keys], NT, preferred_element_type=F32
                )
            for j in range(pairs):
                two = [found[qb, 2 * j], found[qb, 2 * j + 1]]
                both = jnp.concatenate([keys[s, :, head_keys] for s in two], axis=0)
                at = len(columns) * BLK
                scores[:, at : at + 2 * BLK] = lax.dot_general(
                    query, both, NT, preferred_element_type=F32
                )
                columns += two
            spare = jnp.where(n == 2 * pairs, 0.0, LOW)
            acc = [jnp.zeros((BLK, BLK), F32)] * 3
            for g in range(PER):
                top = None
                for j in range(len(columns)):
                    s = scores[g * BLK : (g + 1) * BLK, j * BLK : (j + 1) * BLK]
                    if has_own and j == 0:
                        s = jnp.where(causal, s, LOW)
                    elif j == len(columns) - 1:
                        s = s + spare
                    top = s if top is None else jnp.maximum(top, s)
                peak = jnp.max(top, axis=1, keepdims=True) * TO_LOG2
                total = None
                for j, slot in enumerate(columns):
                    s = scores[g * BLK : (g + 1) * BLK, j * BLK : (j + 1) * BLK]
                    if has_own and j == 0:
                        s = jnp.where(causal, s, LOW)
                    elif j == len(columns) - 1:
                        s = s + spare
                    p = jnp.exp2(s * TO_LOG2 - peak)
                    v = p * reads[slot, pl.ds(k * PER + g, 1), :]
                    total = p if total is None else total + p
                    summed = v if j == 0 else summed + v
                mine = lane == k * PER + g
                for f, x in enumerate(
                    (peak, jnp.sum(total, axis=1, keepdims=True), jnp.sum(summed, axis=1, keepdims=True))
                ):
                    acc[f] = jnp.where(mine, x, acc[f])
            for f in range(3):
                out_ref[f, rows, :] += acc[f]

        def nothing():
            mine = (lane >= k * PER) & (lane < (k + 1) * PER)
            out_ref[0, rows, :] += jnp.where(mine, LOW, 0.0)

        for pairs in range(LIST // 2 + 1):
            if 2 * pairs - 1 > 4 * len(slots):
                continue

            @pl.when((n + 1) // 2 == pairs)
            def _(pairs=pairs):
                if pairs == 0 and not has_own:
                    nothing()
                else:
                    run(pairs)

        return carry

    lax.fori_loop(0, 2 * KVH, step, 0)


def attend(slots, has_own, place, lists, q, msgs):
    blocks = 2 * len(slots)
    return pl.pallas_call(
        lambda *refs: attend_kernel(slots, has_own, *refs),
        out_shape=jax.ShapeDtypeStruct((3, TOK, HD), F32),
        in_specs=[SMEM, SMEM, VMEM] + [VMEM] * len(slots),
        out_specs=VMEM,
        scratch_shapes=[
            pltpu.VMEM((blocks, BLK, HALF), BF16),
            pltpu.VMEM((blocks, HEADS, BLK), F32),
            pltpu.VMEM((PER * BLK, (LIST + 1) * BLK), F32),
            pltpu.SMEM((2, LIST + 1), jnp.int32),
        ],
        compiler_params=pltpu.CompilerParams(vmem_limit_bytes=32 * 1024 * 1024),
        cost_estimate=pl.CostEstimate(
            flops=2 * 2 * HEADS * BLK * HD * BLK * 5, bytes_accessed=4_000_000, transcendentals=5_000_000
        ),
        name="attend",
    )(place, lists, q, *msgs)


def values_kernel(parts, *refs):
    partials, (m_ref, oh_ref, row_ref, col_ref, val_ref, pay_ref) = refs[:parts], refs[parts:]
    top = partials[0][0]
    for x in partials[1:]:
        top = jnp.maximum(top, x[0])
    total = summed = 0.0
    for x in partials:
        w = jnp.exp2(x[0] - top)
        total = total + x[1] * w
        summed = summed + x[2] * w
    lane = iota((TOK, HD), 1)
    share = jnp.where(lane < HEADS, summed / jnp.where(lane < HEADS, total, 1.0), 0.0)
    att = jnp.sum(share, axis=1, keepdims=True)
    diag = iota((TOK, TOK), 0) == iota((TOK, TOK), 1)
    fields = row_ref[...]
    value = fields[0:1] + jnp.sum(jnp.where(diag, att, 0.0), axis=0, keepdims=True)
    val_ref[...] = value
    local = fields[1:2] + jnp.sum(m_ref[...] * att, axis=0, keepdims=True)
    b = jnp.sum(col_ref[...] * att, axis=0, keepdims=True)
    b = fields[5:6] + jnp.concatenate([b, b], axis=1)
    rows = jnp.concatenate([value, local, fields[2:5], b, fields[6:8]], axis=0)
    split = jnp.concatenate(three(rows), axis=0)
    moved = jnp.dot(split, oh_ref[...], preferred_element_type=F32)
    moved = moved[0:8] + moved[8:16] + moved[16:24]
    pay_ref[...] = jnp.zeros_like(pay_ref)
    for g in range(8):
        pay_ref[g, :, 0:32] = moved[:, g * 32 : (g + 1) * 32]


def token_part(partials, m, onehot, rows, cols):
    return pl.pallas_call(
        lambda *refs: values_kernel(len(partials), *refs),
        out_shape=(
            jax.ShapeDtypeStruct((1, TOK), F32),
            jax.ShapeDtypeStruct((8, 8, HD), F32),
        ),
        in_specs=[VMEM] * (len(partials) + 4),
        out_specs=(VMEM, VMEM),
        cost_estimate=pl.CostEstimate(flops=2_000_000, bytes_accessed=1_500_000, transcendentals=65_000),
        name="token_part",
    )(*partials, m, onehot, rows, cols)


def sort_kernel(in_ref, out_ref):
    seqs = iota((64, HD), 0)
    lane = iota((64, HD), 1)
    before = jnp.where(iota((HD, HD), 0) < iota((HD, HD), 1), 1.0, 0.0).astype(BF16)
    ahead = jnp.zeros((64, 1), F32)
    onehots, fields = [], []
    known = jnp.zeros((1, HD), F32)
    lane_row = iota((1, HD), 1)
    zero = jnp.zeros((1, HD), F32)
    for g in range(8):
        x = in_ref[g]
        tag = x[3:4].astype(jnp.int32)
        hit = (seqs == tag) & (lane < 32)
        one = jnp.where(hit, 1.0, 0.0)
        onehot = one.astype(BF16)
        counts = jnp.dot(onehot, before, preferred_element_type=F32) + ahead
        rank = jnp.sum(one * counts, axis=0, keepdims=True)
        ahead = ahead + jnp.sum(one, axis=1, keepdims=True)
        group = jnp.full((1, HD), float(g), F32)
        rows = [
            jnp.where(rank == float(r), f, zero)
            for f in (x[0:1], x[1:2], x[2:3], group)
            for r in range(4)
        ]
        onehots.append(onehot)
        fields.append(jnp.concatenate(rows, axis=0))
        known = jnp.where(lane_row == 16 + g, x[4:5, 0:1], known)
        known = jnp.where(lane_row == 24 + g, x[5:6, 0:1], known)
    table = jnp.concatenate(fields, axis=1)
    table = jnp.concatenate([table, jnp.zeros((HD - 16, 8 * HD), F32)], axis=0)
    onehot = jnp.concatenate(onehots, axis=1)
    moved = 0.0
    for part in three(table):
        moved = moved + lax.dot_general(onehot, part, NT, preferred_element_type=F32)
    out_ref[...] = moved + known


def sort_part(received):
    return pl.pallas_call(
        sort_kernel,
        out_shape=jax.ShapeDtypeStruct((64, HD), F32),
        in_specs=[VMEM],
        out_specs=VMEM,
        cost_estimate=pl.CostEstimate(flops=10_000_000, bytes_accessed=70_000, transcendentals=0),
        name="sort_part",
    )(received)


def finish_kernel(in_ref, adv_ref, ret_ref):
    x = in_ref[...]
    seqs = iota((64, HD), 0)
    lane = iota((64, HD), 1)
    factor = x
    offset = pltpu.roll(x, HD - 8, axis=1)
    span = 1
    while span < 64:
        inside = seqs < 64 - span
        next_factor = jnp.where(inside, pltpu.roll(factor, 64 - span, axis=0), 1.0)
        next_offset = jnp.where(inside, pltpu.roll(offset, 64 - span, axis=0), 0.0)
        offset = offset + factor * next_offset
        factor = factor * next_factor
        span *= 2
    incoming = jnp.where(seqs < 63, pltpu.roll(offset, 63, axis=0), 0.0)
    wide = (64, TOK)
    spot = iota(wide, 1) - 4 * iota(wide, 0)
    adv = jnp.zeros(wide, F32)
    ret = jnp.zeros(wide, F32)
    for r in range(4):
        group = x[:, 12 + r : 13 + r].astype(jnp.int32)
        entry = jnp.sum(jnp.where(lane == group + 16, incoming, 0.0), axis=1, keepdims=True)
        returns = x[:, 4 + r : 5 + r] + x[:, 8 + r : 9 + r] * entry
        advantage = returns - x[:, r : r + 1]
        adv = jnp.where(spot == r, advantage, adv)
        ret = jnp.where(spot == r, returns, ret)
    adv_ref[...] = jnp.sum(adv, axis=0, keepdims=True)
    ret_ref[...] = jnp.sum(ret, axis=0, keepdims=True)


def finish(arrived):
    return pl.pallas_call(
        finish_kernel,
        out_shape=(jax.ShapeDtypeStruct((1, TOK), F32),) * 2,
        in_specs=[VMEM],
        out_specs=(VMEM, VMEM),
        cost_estimate=pl.CostEstimate(flops=500_000, bytes_accessed=40_000, transcendentals=0),
        name="finish",
    )(arrived)


def forward(value, distance, count):
    return lax.ppermute(value, "seq", [(s, s + distance) for s in range(count - distance)])


def swap(value, count):
    return lax.ppermute(value, "seq", [(s, s ^ 1) for s in range(count)])


def shards(queries, keys_values, block_list, value_dir, base_values, rewards, turn_start, actor_shard):
    count = lax.axis_size("seq")
    shard = lax.axis_index("seq").astype(jnp.int32)
    place = shard[None]
    own = message(keys_values[0], value_dir.reshape(HEADS, HD))
    a = forward(own, 2, count)
    b = forward(a, 2, count)
    wa = swap(a, count)
    c = forward(b, 2, count)
    wb = swap(b, count)
    wc = swap(c, count)
    far = [(s, s + 1) for s in range(1, count - 1, 2)]
    near = [(s, s + 1) for s in range(0, count, 2)]
    x = lax.ppermute(jnp.where(shard % 2 == 0, own, c), "seq", far + near)
    m, onehot, rows, cols = weights(place, rewards, turn_start, base_values, actor_shard)
    q, lists = queries[0], block_list[0]
    part = attend((0, 1, 2, 3, 4, 5, 6, 7), True, place, lists, q, (own, a, b, c, x, wa, wb, wc))
    values, payload = token_part((part,), m, onehot, rows, cols)
    received = lax.all_to_all(payload, "group", split_axis=0, concat_axis=0, tiled=True)
    arranged = sort_part(received)
    arrived = lax.all_to_all(arranged, "seq", split_axis=0, concat_axis=0, tiled=True)
    advantage, returns = finish(arrived)
    return values, advantage.reshape(TOK), returns.reshape(TOK)


def solution(mesh):
    placed = (
        P("group", "seq", None),
        P("group", "seq", None),
        P("group", "seq", None),
        P(),
        P("group", "seq"),
        P("group", "seq"),
        P("group", "seq"),
        P("group", "seq"),
    )
    return jax.shard_map(
        shards,
        mesh=mesh,
        in_specs=placed,
        out_specs=(P("group", "seq"), P(("seq", "group")), P(("seq", "group"))),
        check_vma=False,
    )
```

```python
import math

import jax
import jax.numpy as jnp
from jax import lax
from jax.experimental import pallas as pl
from jax.experimental.pallas import tpu as pltpu
from jax.sharding import PartitionSpec as P

HD = 128
BLK = 128
TOK = 256
KVH = 4
HEADS = 32
PER = HEADS // KVH
HALF = KVH * HD
KEYS = KVH // 2
LIST = 8
LATE = 5
MSG = TOK + HEADS // 2
TRACE = 0.995
LOG_TRACE = math.log(TRACE)
TO_LOG2 = HD ** -0.5 * math.log2(math.e)
LOW = -1e30
F32 = jnp.float32
BF16 = jnp.bfloat16

NT = (((1,), (1,)), ((), ()))
SMEM = pl.BlockSpec(memory_space=pltpu.SMEM)
VMEM = pl.BlockSpec(memory_space=pltpu.VMEM)
ANY = pl.BlockSpec(memory_space=pl.ANY)


def iota(shape, dim):
    return lax.broadcasted_iota(jnp.int32, shape, dim)


def three(x):
    first = x.astype(BF16)
    rest = x - first.astype(F32)
    second = rest.astype(BF16)
    third = (rest - second.astype(F32)).astype(BF16)
    return first, second, third


def message_kernel(kv_ref, dir_ref, out_ref):
    out_ref[0:TOK, :] = kv_ref[:, 0:HALF]
    direction = dir_ref[...]
    head = iota((HEADS, HD), 0)
    zero = jnp.zeros_like(direction)
    spread = jnp.concatenate(
        [jnp.where(head // PER == k, direction, zero) for k in range(KVH)], axis=1
    )
    read = lax.dot_general(
        spread, kv_ref[:, HALF:], NT, preferred_element_type=F32
    ).astype(BF16)
    out_ref[TOK:MSG, 0:TOK] = read[0 : HEADS // 2]
    out_ref[TOK:MSG, TOK:HALF] = read[HEADS // 2 :]


def message(kv, direction):
    return pl.pallas_call(
        message_kernel,
        out_shape=jax.ShapeDtypeStruct((MSG, HALF), BF16),
        in_specs=[VMEM, VMEM],
        out_specs=VMEM,
        cost_estimate=pl.CostEstimate(
            flops=2 * TOK * HALF * HEADS, bytes_accessed=800_000, transcendentals=0
        ),
        name="message",
    )(kv, direction)


def weights(shard, rew_ref, turn_ref, base_ref, dest_ref):
    sub, lane = iota((TOK, TOK), 0), iota((TOK, TOK), 1)
    diag = sub == lane

    def column(row):
        return jnp.sum(jnp.where(diag, row, 0.0), axis=1, keepdims=True)

    spot = iota((1, TOK), 1)
    begins = (turn_ref[...] == 1) | ((shard == 0) & (spot == 0))
    start_row = jnp.where(begins, 1.0, 0.0)
    start_col = column(start_row)
    c_row = jnp.sum(jnp.where(sub <= lane, start_col, 0.0), axis=0, keepdims=True)
    c_col = jnp.sum(jnp.where(lane <= sub, start_row, 0.0), axis=1, keepdims=True)
    rewards = column(rew_ref[...])
    base = column(base_ref[...])
    gap = c_col - c_row
    opens = start_col > 0.5
    m = jnp.where((sub > lane) & opens, (1.0 - TRACE) * jnp.exp((gap - 1.0) * LOG_TRACE), 0.0)
    decay = jnp.where(sub >= lane, jnp.exp(gap * LOG_TRACE), 0.0)
    known = jnp.sum(decay * rewards + m * base, axis=0, keepdims=True)
    total = jnp.sum(start_row, axis=1, keepdims=True)
    b_col = jnp.where(opens, (1.0 - TRACE) * jnp.exp((c_col - 1.0) * LOG_TRACE), 0.0)
    b_row = jnp.sum(jnp.where(diag, b_col, 0.0), axis=0, keepdims=True)
    b_known = jnp.sum(b_col * base + jnp.exp(c_col * LOG_TRACE) * rewards, axis=0, keepdims=True)
    dest = dest_ref[...]
    to_group = lax.rem(dest, 8).astype(F32)
    to_seq = (dest // 8).astype(F32)
    group_col = column(to_group)
    rank = jnp.sum(jnp.where((group_col == to_group) & (lane < sub), 1.0, 0.0), axis=1, keepdims=True)
    slot = (group_col * 32.0 + rank).astype(jnp.int32)
    onehot = jnp.where(slot == lane, 1.0, 0.0).astype(BF16)
    wide = (1, TOK)
    rows = [
        base_ref[...],
        known,
        jnp.exp((total - c_row) * LOG_TRACE),
        to_seq,
        jnp.broadcast_to(jnp.exp(total * LOG_TRACE), wide),
        jnp.broadcast_to(b_known, wide),
        jnp.zeros(wide, F32),
        jnp.zeros(wide, F32),
    ]
    return m, onehot, jnp.concatenate(rows, axis=0), b_row


def attend_kernel(slots, arrays, earlier, place_ref, list_ref, q_ref, *rest):
    count = len(slots)
    has_own = 0 in slots
    msgs, rest = rest[:arrays], rest[arrays:]
    if earlier:
        before_ref, *late_refs = rest[:LATE]
        val_ref, pay_ref, table, score0, score1, found, sems, out_ref = rest[LATE:]
        scores = (score0, score1)
    else:
        out_ref, table, *scores, found, sems = rest
    shard = place_ref[0]
    core = lax.rem(shard, 2)

    copies = []
    sources = [msg.at[at : at + MSG] for msg in msgs for at in range(0, msg.shape[0], MSG)]
    for i, source in enumerate(sources):
        copies.append(pltpu.make_async_copy(source, table.at[i], sems.at[i]))
    for copy in copies:
        copy.start()

    for qb in range(2):
        block = shard * 2 + qb
        n = jnp.int32(0)
        entries = [list_ref[qb, j] for j in range(LIST)]
        for j in range(LIST):
            found[qb, j] = 0
        for j in range(LIST):
            entry = entries[j]
            use = entry < block
            for i in range(j):
                use = use & (entries[i] != entry)
            back = shard - entry // 2
            even = lax.rem(back, 2) == 0
            slot = jnp.where(even, back // 2, 4 + lax.rem(back // 2 + 1 - core, 4))
            local = jnp.int32(0)
            here = jnp.bool_(False)
            for i, s in enumerate(slots):
                hit = slot == s
                local = jnp.where(hit, 2 * i, local)
                here = here | hit
            use = use & here
            at = jnp.minimum(n, LIST - 1)
            found[qb, at] = jnp.where(use, local + lax.rem(entry, 2), found[qb, at])
            n = n + jnp.where(use, 1, 0)
        found[qb, LIST] = n
    out_ref[...] = jnp.zeros_like(out_ref)
    for copy in copies:
        copy.wait()

    causal = iota((BLK, BLK), 1) <= iota((BLK, BLK), 0)
    lane_pair = iota((BLK, 2 * HEADS), 1)
    lane_head = iota((BLK, HEADS), 1)
    ones = jnp.ones((HEADS, BLK), BF16)

    def step(index, carry):
        qb, side = index // 2, lax.rem(index, 2)
        rows = pl.ds(pl.multiple_of(qb * BLK, BLK), BLK)
        n = found[qb, LIST]

        def run(blocks):
            codes = [qb] if has_own else []
            codes += [found[qb, j] for j in range(blocks - len(codes))]
            spots = [(code // 2, pl.multiple_of(lax.rem(code, 2) * BLK, BLK)) for code in codes]
            read = jnp.concatenate(
                [
                    jnp.concatenate(
                        [
                            table[i, TOK:MSG, pl.ds(at, BLK)],
                            table[i, TOK:MSG, pl.ds(pl.multiple_of(at + TOK, BLK), BLK)],
                        ],
                        axis=0,
                    )
                    for i, at in spots
                ],
                axis=1,
            )
            read = jnp.concatenate([read, jnp.concatenate([ones] * blocks, axis=1)], axis=0)
            spare = jnp.where(n + has_own == blocks, 0.0, LOW)
            for k in range(KEYS):
                first = (side * KEYS + k) * PER * HD
                heads = [q_ref[rows, pl.ds(pl.multiple_of(first + g * HD, HD), HD)] for g in range(PER)]
                query = jnp.concatenate(heads, axis=0)
                own = pl.ds(pl.multiple_of((side * KEYS + k) * HD, HD), HD)
                for j in range(0, blocks, 2):
                    both = jnp.concatenate([table[i, pl.ds(at, BLK), own] for i, at in spots[j : j + 2]], axis=0)
                    scores[k][:, j * BLK : (j + 2) * BLK] = lax.dot_general(
                        query, both, NT, preferred_element_type=F32
                    )
            sums = jnp.zeros((BLK, 2 * HEADS), F32)
            peaks = jnp.zeros((BLK, HEADS), F32)
            for k in range(KEYS):
                for g in range(PER):
                    parts = []
                    for j in range(blocks):
                        s = scores[k][g * BLK : (g + 1) * BLK, j * BLK : (j + 1) * BLK]
                        if has_own and j == 0:
                            s = jnp.where(causal, s, LOW)
                        elif j == blocks - 1:
                            s = s + spare
                        parts.append(s)
                    top = parts[0]
                    for s in parts[1:]:
                        top = jnp.maximum(top, s)
                    peak = jnp.max(top, axis=1, keepdims=True) * TO_LOG2
                    p = jnp.concatenate([jnp.exp2(s * TO_LOG2 - peak).astype(BF16) for s in parts], axis=1)
                    both = lax.dot_general(p, read, NT, preferred_element_type=F32)
                    head = (side * KEYS + k) * PER + g
                    sums = jnp.where((lane_pair == head) | (lane_pair == head + HEADS), both, sums)
                    peaks = jnp.where(lane_head == head, peak, peaks)
            out_ref[0, rows, 0 : 2 * HEADS] += sums
            out_ref[1, rows, 0:HEADS] += peaks

        def nothing():
            mine = lane_head // (HEADS // 2) == side
            out_ref[1, rows, 0:HEADS] += jnp.where(mine, LOW, 0.0)

        most = min(LIST, 2 * count) + has_own
        for pairs in range((most + 1) // 2 + 1):
            if pairs == 0 and has_own:
                continue

            @pl.when((n + has_own + 1) // 2 == pairs)
            def _(pairs=pairs):
                if pairs:
                    run(2 * pairs)
                else:
                    nothing()

        return carry

    lax.fori_loop(0, 4, step, 0)

    if earlier:
        every = [out_ref, before_ref]
        peaks = [ref[1, :, 0:HEADS] for ref in every]
        top = peaks[0]
        for peak in peaks[1:]:
            top = jnp.maximum(top, peak)
        total = summed = 0.0
        for ref, peak in zip(every, peaks):
            weight = jnp.exp2(peak - top)
            total = total + ref[0, :, HEADS : 2 * HEADS] * weight
            summed = summed + ref[0, :, 0:HEADS] * weight
        att = jnp.sum(summed / total, axis=1, keepdims=True)
        diag = iota((TOK, TOK), 0) == iota((TOK, TOK), 1)
        m, onehot, fields, b_row = weights(shard, *late_refs)
        att_row = jnp.sum(jnp.where(diag, att, 0.0), axis=0, keepdims=True)
        value = fields[0:1] + att_row
        val_ref[...] = value
        local = fields[1:2] + jnp.sum(m * att, axis=0, keepdims=True)
        b = fields[5:6] + jnp.sum(b_row * att_row, axis=1, keepdims=True)
        lines = jnp.concatenate([value, local, fields[2:5], b, fields[6:8]], axis=0)
        split = jnp.concatenate(three(lines), axis=0)
        moved = jnp.dot(split, onehot, preferred_element_type=F32)
        moved = moved[0:8] + moved[8:16] + moved[16:24]
        pay_ref[...] = jnp.zeros_like(pay_ref)
        for g in range(8):
            pay_ref[g, :, 0:32] = moved[:, g * 32 : (g + 1) * 32]


def attend(slots, place, lists, q, msgs, befores=(), extra=()):
    count = len(slots)
    partial = (2, TOK, BLK)
    most = min(LIST, 2 * count) + 2
    scratch = [
        pltpu.VMEM((count, MSG, HALF), BF16),
        pltpu.VMEM((PER * BLK, most * BLK), F32),
        pltpu.VMEM((PER * BLK, most * BLK), F32),
        pltpu.SMEM((2, LIST + 1), jnp.int32),
        pltpu.SemaphoreType.DMA((count,)),
    ]
    late = ()
    if befores:
        out_shape = (jax.ShapeDtypeStruct((1, TOK), F32), jax.ShapeDtypeStruct((8, 8, HD), F32))
        out_specs = (VMEM, VMEM)
        late = (*befores, *extra)
        scratch.append(pltpu.VMEM(partial, F32))
    else:
        out_shape, out_specs = jax.ShapeDtypeStruct(partial, F32), VMEM
    return pl.pallas_call(
        lambda *refs: attend_kernel(slots, len(msgs), len(befores), *refs),
        out_shape=out_shape,
        in_specs=[SMEM, SMEM, VMEM] + [ANY] * len(msgs) + [VMEM] * len(late),
        out_specs=out_specs,
        scratch_shapes=scratch,
        compiler_params=pltpu.CompilerParams(vmem_limit_bytes=32 * 1024 * 1024),
        cost_estimate=pl.CostEstimate(
            flops=1_000_000, bytes_accessed=100_000, transcendentals=0
        ),
        name="attend",
    )(place, lists, q, *msgs, *late)


def sort_kernel(in_ref, out_ref):
    seqs = iota((64, HD), 0)
    lane = iota((64, HD), 1)
    before = jnp.where(iota((HD, HD), 0) < iota((HD, HD), 1), 1.0, 0.0).astype(BF16)
    ahead = jnp.zeros((64, 1), F32)
    onehots, fields = [], []
    known = jnp.zeros((1, HD), F32)
    lane_row = iota((1, HD), 1)
    zero = jnp.zeros((1, HD), F32)
    for g in range(8):
        x = in_ref[g]
        tag = x[3:4].astype(jnp.int32)
        hit = (seqs == tag) & (lane < 32)
        one = jnp.where(hit, 1.0, 0.0)
        onehot = one.astype(BF16)
        counts = jnp.dot(onehot, before, preferred_element_type=F32) + ahead
        rank = jnp.sum(one * counts, axis=0, keepdims=True)
        ahead = ahead + jnp.sum(one, axis=1, keepdims=True)
        group = jnp.full((1, HD), float(g), F32)
        rows = [
            jnp.where(rank == float(r), f, zero)
            for f in (x[0:1], x[1:2], x[2:3], group)
            for r in range(4)
        ]
        onehots.append(onehot)
        fields.append(jnp.concatenate(rows, axis=0))
        known = jnp.where(lane_row == 16 + g, x[4:5, 0:1], known)
        known = jnp.where(lane_row == 24 + g, x[5:6, 0:1], known)
    table = jnp.concatenate(fields, axis=1)
    table = jnp.concatenate([table, jnp.zeros((HD - 16, 8 * HD), F32)], axis=0)
    onehot = jnp.concatenate(onehots, axis=1)
    moved = 0.0
    for part in three(table):
        moved = moved + lax.dot_general(onehot, part, NT, preferred_element_type=F32)
    out_ref[...] = moved + known


def sort_part(received):
    return pl.pallas_call(
        sort_kernel,
        out_shape=jax.ShapeDtypeStruct((64, HD), F32),
        in_specs=[VMEM],
        out_specs=VMEM,
        cost_estimate=pl.CostEstimate(flops=10_000_000, bytes_accessed=70_000, transcendentals=0),
        name="sort_part",
    )(received)


def finish_kernel(in_ref, adv_ref, ret_ref):
    x = in_ref[...]
    seqs = iota((64, HD), 0)
    lane = iota((64, HD), 1)
    factor = x
    offset = pltpu.roll(x, HD - 8, axis=1)
    span = 1
    while span < 64:
        inside = seqs < 64 - span
        next_factor = jnp.where(inside, pltpu.roll(factor, 64 - span, axis=0), 1.0)
        next_offset = jnp.where(inside, pltpu.roll(offset, 64 - span, axis=0), 0.0)
        offset = offset + factor * next_offset
        factor = factor * next_factor
        span *= 2
    incoming = jnp.where(seqs < 63, pltpu.roll(offset, 63, axis=0), 0.0)
    wide = (64, TOK)
    spot = iota(wide, 1) - 4 * iota(wide, 0)
    adv = jnp.zeros(wide, F32)
    ret = jnp.zeros(wide, F32)
    for r in range(4):
        group = x[:, 12 + r : 13 + r].astype(jnp.int32)
        entry = jnp.sum(jnp.where(lane == group + 16, incoming, 0.0), axis=1, keepdims=True)
        returns = x[:, 4 + r : 5 + r] + x[:, 8 + r : 9 + r] * entry
        advantage = returns - x[:, r : r + 1]
        adv = jnp.where(spot == r, advantage, adv)
        ret = jnp.where(spot == r, returns, ret)
    adv_ref[...] = jnp.sum(adv, axis=0, keepdims=True)
    ret_ref[...] = jnp.sum(ret, axis=0, keepdims=True)


def finish(arrived):
    return pl.pallas_call(
        finish_kernel,
        out_shape=(jax.ShapeDtypeStruct((1, TOK), F32),) * 2,
        in_specs=[VMEM],
        out_specs=(VMEM, VMEM),
        cost_estimate=pl.CostEstimate(flops=500_000, bytes_accessed=40_000, transcendentals=0),
        name="finish",
    )(arrived)


YS = 8


def swap(value, count):
    return lax.ppermute(value, "seq", [(s, s ^ 1) for s in range(count)])


def hop(value, chips, count):
    return lax.ppermute(value, "seq", [(s, s + 2 * chips) for s in range(count - 2 * chips)])


def place_of(x, y, core):
    return (x * YS + y) * 2 + core


def shards(queries, keys_values, block_list, value_dir, base_values, rewards, turn_start, actor_shard):
    count = lax.axis_size("seq")
    shard = lax.axis_index("seq").astype(jnp.int32)
    place = shard[None]
    core = shard % 2
    heads = (place, block_list[0], queries[0])
    own = message(keys_values[0], value_dir.reshape(HEADS, HD))
    a = hop(own, 1, count)
    b = hop(own, 2, count)
    back, last = [], []
    for s in range(count):
        x, y = s // (2 * YS), s // 2 % YS
        if s % 2 == 0:
            last.append((s, s + 1))
        elif s + 7 < count:
            between = place_of(x, (y - 2) % YS, 1)
            back.append((s, between))
            last.append((between, s + 7))
    relayed = lax.ppermute(own, "seq", back)
    sums0 = attend((0, 1), *heads, (own, a))
    sent = jnp.where(core == 0, own, relayed)
    a, b, sent, sums0 = lax.optimization_barrier((a, b, sent, sums0))
    c = hop(b, 1, count)
    far = lax.ppermute(sent, "seq", last)
    wab = swap(jnp.concatenate([a, b], axis=0), count)
    wc = swap(c, count)
    extra = (rewards, turn_start, base_values, actor_shard)
    values, payload = attend((5, 6, 2, 4, 3, 7), *heads, (wab, b, far, c, wc), (sums0,), extra)
    received = lax.all_to_all(payload, "group", split_axis=0, concat_axis=0, tiled=True)
    arranged = sort_part(received)
    arrived = lax.all_to_all(arranged, "seq", split_axis=0, concat_axis=0, tiled=True)
    advantage, returns = finish(arrived)
    return values, advantage.reshape(TOK), returns.reshape(TOK)


def solution(mesh):
    placed = (
        P("group", "seq", None),
        P("group", "seq", None),
        P("group", "seq", None),
        P(),
        P("group", "seq"),
        P("group", "seq"),
        P("group", "seq"),
        P("group", "seq"),
    )
    return jax.shard_map(
        shards,
        mesh=mesh,
        in_specs=placed,
        out_specs=(P("group", "seq"), P(("seq", "group")), P(("seq", "group"))),
        check_vma=False,
    )
```

```python
import math

import jax
import jax.numpy as jnp
from jax import lax
from jax.experimental import pallas as pl
from jax.experimental.pallas import tpu as pltpu
from jax.sharding import PartitionSpec as P

HD = 128
BLK = 128
TOK = 256
KVH = 4
HEADS = 32
PER = HEADS // KVH
HALF = KVH * HD
KEYS = KVH // 2
LIST = 8
LATE = 5
MSG = TOK + HEADS // 2
TRACE = 0.995
LOG_TRACE = math.log(TRACE)
TO_LOG2 = HD ** -0.5 * math.log2(math.e)
LOW = -1e30
F32 = jnp.float32
BF16 = jnp.bfloat16

NT = (((1,), (1,)), ((), ()))
SMEM = pl.BlockSpec(memory_space=pltpu.SMEM)
VMEM = pl.BlockSpec(memory_space=pltpu.VMEM)
ANY = pl.BlockSpec(memory_space=pl.ANY)


def iota(shape, dim):
    return lax.broadcasted_iota(jnp.int32, shape, dim)


def three(x):
    first = x.astype(BF16)
    rest = x - first.astype(F32)
    second = rest.astype(BF16)
    third = (rest - second.astype(F32)).astype(BF16)
    return first, second, third


def message_kernel(kv_ref, dir_ref, out_ref):
    out_ref[0:TOK, :] = kv_ref[:, 0:HALF]
    direction = dir_ref[...]
    head = iota((HEADS, HD), 0)
    zero = jnp.zeros_like(direction)
    spread = jnp.concatenate(
        [jnp.where(head // PER == k, direction, zero) for k in range(KVH)], axis=1
    )
    read = lax.dot_general(
        spread, kv_ref[:, HALF:], NT, preferred_element_type=F32
    ).astype(BF16)
    out_ref[TOK:MSG, 0:TOK] = read[0 : HEADS // 2]
    out_ref[TOK:MSG, TOK:HALF] = read[HEADS // 2 :]


def message(kv, direction):
    return pl.pallas_call(
        message_kernel,
        out_shape=jax.ShapeDtypeStruct((MSG, HALF), BF16),
        in_specs=[VMEM, VMEM],
        out_specs=VMEM,
        cost_estimate=pl.CostEstimate(
            flops=2 * TOK * HALF * HEADS, bytes_accessed=800_000, transcendentals=0
        ),
        name="message",
    )(kv, direction)


def weights(shard, rew_ref, turn_ref, base_ref, dest_ref):
    sub, lane = iota((TOK, TOK), 0), iota((TOK, TOK), 1)
    diag = sub == lane

    def column(row):
        return jnp.sum(jnp.where(diag, row, 0.0), axis=1, keepdims=True)

    spot = iota((1, TOK), 1)
    begins = (turn_ref[...] == 1) | ((shard == 0) & (spot == 0))
    start_row = jnp.where(begins, 1.0, 0.0)
    start_col = column(start_row)
    c_row = jnp.sum(jnp.where(sub <= lane, start_col, 0.0), axis=0, keepdims=True)
    c_col = jnp.sum(jnp.where(lane <= sub, start_row, 0.0), axis=1, keepdims=True)
    rewards = column(rew_ref[...])
    base = column(base_ref[...])
    gap = c_col - c_row
    opens = start_col > 0.5
    m = jnp.where((sub > lane) & opens, (1.0 - TRACE) * jnp.exp((gap - 1.0) * LOG_TRACE), 0.0)
    decay = jnp.where(sub >= lane, jnp.exp(gap * LOG_TRACE), 0.0)
    known = jnp.sum(decay * rewards + m * base, axis=0, keepdims=True)
    total = jnp.sum(start_row, axis=1, keepdims=True)
    b_col = jnp.where(opens, (1.0 - TRACE) * jnp.exp((c_col - 1.0) * LOG_TRACE), 0.0)
    b_row = jnp.sum(jnp.where(diag, b_col, 0.0), axis=0, keepdims=True)
    b_known = jnp.sum(b_col * base + jnp.exp(c_col * LOG_TRACE) * rewards, axis=0, keepdims=True)
    dest = dest_ref[...]
    to_group = lax.rem(dest, 8).astype(F32)
    to_seq = (dest // 8).astype(F32)
    group_col = column(to_group)
    rank = jnp.sum(jnp.where((group_col == to_group) & (lane < sub), 1.0, 0.0), axis=1, keepdims=True)
    slot = (group_col * 32.0 + rank).astype(jnp.int32)
    onehot = jnp.where(slot == lane, 1.0, 0.0).astype(BF16)
    wide = (1, TOK)
    rows = [
        base_ref[...],
        known,
        jnp.exp((total - c_row) * LOG_TRACE),
        to_seq,
        jnp.broadcast_to(jnp.exp(total * LOG_TRACE), wide),
        jnp.broadcast_to(b_known, wide),
        jnp.zeros(wide, F32),
        jnp.zeros(wide, F32),
    ]
    return m, onehot, jnp.concatenate(rows, axis=0), b_row


def attend_kernel(slots, arrays, earlier, place_ref, list_ref, q_ref, *rest):
    count = len(slots)
    has_own = 0 in slots
    msgs, rest = rest[:arrays], rest[arrays:]
    if earlier:
        before_ref, *late_refs = rest[:LATE]
        val_ref, pay_ref, table, score0, score1, found, sems, out_ref = rest[LATE:]
        scores = (score0, score1)
    else:
        out_ref, table, *scores, found, sems = rest
    shard = place_ref[0]
    core = lax.rem(shard, 2)

    copies = []
    sources = [msg.at[at : at + MSG] for msg in msgs for at in range(0, msg.shape[0], MSG)]
    for i, source in enumerate(sources):
        copies.append(pltpu.make_async_copy(source, table.at[i], sems.at[i]))
    for copy in copies:
        copy.start()

    for qb in range(2):
        block = shard * 2 + qb
        n = jnp.int32(0)
        entries = [list_ref[qb, j] for j in range(LIST)]
        for j in range(LIST):
            found[qb, j] = 0
        for j in range(LIST):
            entry = entries[j]
            use = entry < block
            for i in range(j):
                use = use & (entries[i] != entry)
            back = shard - entry // 2
            even = lax.rem(back, 2) == 0
            slot = jnp.where(even, back // 2, 4 + lax.rem(back // 2 + 1 - core, 4))
            local = jnp.int32(0)
            here = jnp.bool_(False)
            for i, s in enumerate(slots):
                hit = slot == s
                local = jnp.where(hit, 2 * i, local)
                here = here | hit
            use = use & here
            at = jnp.minimum(n, LIST - 1)
            found[qb, at] = jnp.where(use, local + lax.rem(entry, 2), found[qb, at])
            n = n + jnp.where(use, 1, 0)
        found[qb, LIST] = n
    out_ref[...] = jnp.zeros_like(out_ref)
    if earlier:
        m, onehot, fields, b_row = weights(shard, *late_refs)
    for copy in copies:
        copy.wait()

    causal = iota((BLK, BLK), 1) <= iota((BLK, BLK), 0)
    lane_pair = iota((BLK, 2 * HEADS), 1)
    lane_head = iota((BLK, HEADS), 1)
    ones = jnp.ones((HEADS, BLK), BF16)

    def step(index, carry):
        qb, side = index // 2, lax.rem(index, 2)
        rows = pl.ds(pl.multiple_of(qb * BLK, BLK), BLK)
        n = found[qb, LIST]

        def run(blocks):
            codes = [qb] if has_own else []
            codes += [found[qb, j] for j in range(blocks - len(codes))]
            spots = [(code // 2, pl.multiple_of(lax.rem(code, 2) * BLK, BLK)) for code in codes]
            read = jnp.concatenate(
                [
                    jnp.concatenate(
                        [
                            table[i, TOK:MSG, pl.ds(at, BLK)],
                            table[i, TOK:MSG, pl.ds(pl.multiple_of(at + TOK, BLK), BLK)],
                        ],
                        axis=0,
                    )
                    for i, at in spots
                ],
                axis=1,
            )
            read = jnp.concatenate([read, jnp.concatenate([ones] * blocks, axis=1)], axis=0)
            for k in range(KEYS):
                first = (side * KEYS + k) * PER * HD
                heads = [q_ref[rows, pl.ds(pl.multiple_of(first + g * HD, HD), HD)] for g in range(PER)]
                query = jnp.concatenate(heads, axis=0)
                own = pl.ds(pl.multiple_of((side * KEYS + k) * HD, HD), HD)
                for j in range(0, blocks, 2):
                    both = jnp.concatenate([table[i, pl.ds(at, BLK), own] for i, at in spots[j : j + 2]], axis=0)
                    scores[k][:, j * BLK : min(j + 2, blocks) * BLK] = lax.dot_general(
                        query, both, NT, preferred_element_type=F32
                    )
            sums = jnp.zeros((BLK, 2 * HEADS), F32)
            peaks = jnp.zeros((BLK, HEADS), F32)
            for k in range(KEYS):
                for g in range(PER):
                    parts = []
                    for j in range(blocks):
                        s = scores[k][g * BLK : (g + 1) * BLK, j * BLK : (j + 1) * BLK]
                        if has_own and j == 0:
                            s = jnp.where(causal, s, LOW)
                        parts.append(s)
                    top = parts[0]
                    for s in parts[1:]:
                        top = jnp.maximum(top, s)
                    peak = jnp.max(top, axis=1, keepdims=True) * TO_LOG2
                    p = jnp.concatenate([jnp.exp2(s * TO_LOG2 - peak).astype(BF16) for s in parts], axis=1)
                    both = lax.dot_general(p, read, NT, preferred_element_type=F32)
                    head = (side * KEYS + k) * PER + g
                    sums = jnp.where((lane_pair == head) | (lane_pair == head + HEADS), both, sums)
                    peaks = jnp.where(lane_head == head, peak, peaks)
            out_ref[0, rows, 0 : 2 * HEADS] += sums
            out_ref[1, rows, 0:HEADS] += peaks

        def nothing():
            mine = lane_head // (HEADS // 2) == side
            out_ref[1, rows, 0:HEADS] += jnp.where(mine, LOW, 0.0)

        for others in range(min(LIST, 2 * count) + 1):

            @pl.when(n == others)
            def _(others=others):
                if others + has_own:
                    run(others + has_own)
                else:
                    nothing()

        return carry

    lax.fori_loop(0, 4, step, 0)

    if earlier:
        every = [out_ref, before_ref]
        peaks = [ref[1, :, 0:HEADS] for ref in every]
        top = peaks[0]
        for peak in peaks[1:]:
            top = jnp.maximum(top, peak)
        total = summed = 0.0
        for ref, peak in zip(every, peaks):
            weight = jnp.exp2(peak - top)
            total = total + ref[0, :, HEADS : 2 * HEADS] * weight
            summed = summed + ref[0, :, 0:HEADS] * weight
        att = jnp.sum(summed / total, axis=1, keepdims=True)
        diag = iota((TOK, TOK), 0) == iota((TOK, TOK), 1)
        att_row = jnp.sum(jnp.where(diag, att, 0.0), axis=0, keepdims=True)
        value = fields[0:1] + att_row
        val_ref[...] = value
        local = fields[1:2] + jnp.sum(m * att, axis=0, keepdims=True)
        b = fields[5:6] + jnp.sum(b_row * att_row, axis=1, keepdims=True)
        lines = jnp.concatenate([value, local, fields[2:5], b, fields[6:8]], axis=0)
        split = jnp.concatenate(three(lines), axis=0)
        moved = jnp.dot(split, onehot, preferred_element_type=F32)
        moved = moved[0:8] + moved[8:16] + moved[16:24]
        pay_ref[...] = jnp.zeros_like(pay_ref)
        for g in range(8):
            pay_ref[g, :, 0:32] = moved[:, g * 32 : (g + 1) * 32]


def attend(slots, place, lists, q, msgs, befores=(), extra=()):
    count = len(slots)
    partial = (2, TOK, BLK)
    most = min(LIST, 2 * count) + (0 in slots)
    scratch = [
        pltpu.VMEM((count, MSG, HALF), BF16),
        pltpu.VMEM((PER * BLK, most * BLK), F32),
        pltpu.VMEM((PER * BLK, most * BLK), F32),
        pltpu.SMEM((2, LIST + 1), jnp.int32),
        pltpu.SemaphoreType.DMA((count,)),
    ]
    late = ()
    if befores:
        out_shape = (jax.ShapeDtypeStruct((1, TOK), F32), jax.ShapeDtypeStruct((8, 8, HD), F32))
        out_specs = (VMEM, VMEM)
        late = (*befores, *extra)
        scratch.append(pltpu.VMEM(partial, F32))
    else:
        out_shape, out_specs = jax.ShapeDtypeStruct(partial, F32), VMEM
    return pl.pallas_call(
        lambda *refs: attend_kernel(slots, len(msgs), len(befores), *refs),
        out_shape=out_shape,
        in_specs=[SMEM, SMEM, VMEM] + [ANY] * len(msgs) + [VMEM] * len(late),
        out_specs=out_specs,
        scratch_shapes=scratch,
        compiler_params=pltpu.CompilerParams(vmem_limit_bytes=32 * 1024 * 1024),
        cost_estimate=pl.CostEstimate(
            flops=1_000_000, bytes_accessed=100_000, transcendentals=0
        ),
        name="attend",
    )(place, lists, q, *msgs, *late)


def sort_kernel(in_ref, out_ref):
    seqs = iota((64, HD), 0)
    lane = iota((64, HD), 1)
    before = jnp.where(iota((HD, HD), 0) < iota((HD, HD), 1), 1.0, 0.0).astype(BF16)
    ahead = jnp.zeros((64, 1), F32)
    onehots, fields = [], []
    known = jnp.zeros((1, HD), F32)
    lane_row = iota((1, HD), 1)
    zero = jnp.zeros((1, HD), F32)
    for g in range(8):
        x = in_ref[g]
        tag = x[3:4].astype(jnp.int32)
        hit = (seqs == tag) & (lane < 32)
        one = jnp.where(hit, 1.0, 0.0)
        onehot = one.astype(BF16)
        counts = jnp.dot(onehot, before, preferred_element_type=F32) + ahead
        rank = jnp.sum(one * counts, axis=0, keepdims=True)
        ahead = ahead + jnp.sum(one, axis=1, keepdims=True)
        group = jnp.full((1, HD), float(g), F32)
        rows = [
            jnp.where(rank == float(r), f, zero)
            for f in (x[0:1], x[1:2], x[2:3], group)
            for r in range(4)
        ]
        onehots.append(onehot)
        fields.append(jnp.concatenate(rows, axis=0))
        known = jnp.where(lane_row == 16 + g, x[4:5, 0:1], known)
        known = jnp.where(lane_row == 24 + g, x[5:6, 0:1], known)
    table = jnp.concatenate(fields, axis=1)
    table = jnp.concatenate([table, jnp.zeros((HD - 16, 8 * HD), F32)], axis=0)
    onehot = jnp.concatenate(onehots, axis=1)
    moved = 0.0
    for part in three(table):
        moved = moved + lax.dot_general(onehot, part, NT, preferred_element_type=F32)
    out_ref[...] = moved + known


def sort_part(received):
    return pl.pallas_call(
        sort_kernel,
        out_shape=jax.ShapeDtypeStruct((64, HD), F32),
        in_specs=[VMEM],
        out_specs=VMEM,
        cost_estimate=pl.CostEstimate(flops=10_000_000, bytes_accessed=70_000, transcendentals=0),
        name="sort_part",
    )(received)


def finish_kernel(in_ref, adv_ref, ret_ref):
    x = in_ref[...]
    seqs = iota((64, HD), 0)
    lane = iota((64, HD), 1)
    factor = x
    offset = pltpu.roll(x, HD - 8, axis=1)
    span = 1
    while span < 64:
        inside = seqs < 64 - span
        next_factor = jnp.where(inside, pltpu.roll(factor, 64 - span, axis=0), 1.0)
        next_offset = jnp.where(inside, pltpu.roll(offset, 64 - span, axis=0), 0.0)
        offset = offset + factor * next_offset
        factor = factor * next_factor
        span *= 2
    incoming = jnp.where(seqs < 63, pltpu.roll(offset, 63, axis=0), 0.0)
    wide = (64, TOK)
    spot = iota(wide, 1) - 4 * iota(wide, 0)
    adv = jnp.zeros(wide, F32)
    ret = jnp.zeros(wide, F32)
    for r in range(4):
        group = x[:, 12 + r : 13 + r].astype(jnp.int32)
        entry = jnp.sum(jnp.where(lane == group + 16, incoming, 0.0), axis=1, keepdims=True)
        returns = x[:, 4 + r : 5 + r] + x[:, 8 + r : 9 + r] * entry
        advantage = returns - x[:, r : r + 1]
        adv = jnp.where(spot == r, advantage, adv)
        ret = jnp.where(spot == r, returns, ret)
    adv_ref[...] = jnp.sum(adv, axis=0, keepdims=True)
    ret_ref[...] = jnp.sum(ret, axis=0, keepdims=True)


def finish(arrived):
    return pl.pallas_call(
        finish_kernel,
        out_shape=(jax.ShapeDtypeStruct((1, TOK), F32),) * 2,
        in_specs=[VMEM],
        out_specs=(VMEM, VMEM),
        cost_estimate=pl.CostEstimate(flops=500_000, bytes_accessed=40_000, transcendentals=0),
        name="finish",
    )(arrived)


YS = 8


def swap(value, count):
    return lax.ppermute(value, "seq", [(s, s ^ 1) for s in range(count)])


def hop(value, chips, count):
    return lax.ppermute(value, "seq", [(s, s + 2 * chips) for s in range(count - 2 * chips)])


def place_of(x, y, core):
    return (x * YS + y) * 2 + core


def shards(queries, keys_values, block_list, value_dir, base_values, rewards, turn_start, actor_shard):
    count = lax.axis_size("seq")
    shard = lax.axis_index("seq").astype(jnp.int32)
    place = shard[None]
    core = shard % 2
    heads = (place, block_list[0], queries[0])
    own = message(keys_values[0], value_dir.reshape(HEADS, HD))
    a = hop(own, 1, count)
    b = hop(own, 2, count)
    back, last = [], []
    for s in range(count):
        x, y = s // (2 * YS), s // 2 % YS
        if s % 2 == 0:
            last.append((s, s + 1))
        elif s + 7 < count:
            between = place_of(x, (y - 2) % YS, 1)
            back.append((s, between))
            last.append((between, s + 7))
    relayed = lax.ppermute(own, "seq", back)
    sums0 = attend((0, 1), *heads, (own, a))
    sent = jnp.where(core == 0, own, relayed)
    a, b, sent, sums0 = lax.optimization_barrier((a, b, sent, sums0))
    c = hop(b, 1, count)
    far = lax.ppermute(sent, "seq", last)
    wab = swap(jnp.concatenate([a, b], axis=0), count)
    wc = swap(c, count)
    extra = (rewards, turn_start, base_values, actor_shard)
    values, payload = attend((5, 6, 2, 4, 3, 7), *heads, (wab, b, far, c, wc), (sums0,), extra)
    received = lax.all_to_all(payload, "group", split_axis=0, concat_axis=0, tiled=True)
    arranged = sort_part(received)
    arrived = lax.all_to_all(arranged, "seq", split_axis=0, concat_axis=0, tiled=True)
    advantage, returns = finish(arrived)
    return values, advantage.reshape(TOK), returns.reshape(TOK)


def solution(mesh):
    placed = (
        P("group", "seq", None),
        P("group", "seq", None),
        P("group", "seq", None),
        P(),
        P("group", "seq"),
        P("group", "seq"),
        P("group", "seq"),
        P("group", "seq"),
    )
    return jax.shard_map(
        shards,
        mesh=mesh,
        in_specs=placed,
        out_specs=(P("group", "seq"), P(("seq", "group")), P(("seq", "group"))),
        check_vma=False,
    )
```

```python
import math

import jax
import jax.numpy as jnp
from jax import lax
from jax.experimental import pallas as pl
from jax.experimental.pallas import tpu as pltpu
from jax.sharding import PartitionSpec as P

HD = 128
BLK = 128
TOK = 256
KVH = 4
HEADS = 32
PER = HEADS // KVH
HALF = KVH * HD
KEYS = KVH // 2
LIST = 8
LATE = 5
MSG = TOK + HEADS // 2
TRACE = 0.995
LOG_TRACE = math.log(TRACE)
TO_LOG2 = HD ** -0.5 * math.log2(math.e)
LOW = -1e30
F32 = jnp.float32
BF16 = jnp.bfloat16

NT = (((1,), (1,)), ((), ()))
SMEM = pl.BlockSpec(memory_space=pltpu.SMEM)
VMEM = pl.BlockSpec(memory_space=pltpu.VMEM)
ANY = pl.BlockSpec(memory_space=pl.ANY)


def iota(shape, dim):
    return lax.broadcasted_iota(jnp.int32, shape, dim)


def three(x):
    first = x.astype(BF16)
    rest = x - first.astype(F32)
    second = rest.astype(BF16)
    third = (rest - second.astype(F32)).astype(BF16)
    return first, second, third


def message_kernel(kv_ref, dir_ref, out_ref):
    out_ref[0:TOK, :] = kv_ref[:, 0:HALF]
    direction = dir_ref[...]
    head = iota((HEADS, HD), 0)
    zero = jnp.zeros_like(direction)
    spread = jnp.concatenate(
        [jnp.where(head // PER == k, direction, zero) for k in range(KVH)], axis=1
    )
    read = lax.dot_general(
        spread, kv_ref[:, HALF:], NT, preferred_element_type=F32
    ).astype(BF16)
    out_ref[TOK:MSG, 0:TOK] = read[0 : HEADS // 2]
    out_ref[TOK:MSG, TOK:HALF] = read[HEADS // 2 :]


def message(kv, direction):
    return pl.pallas_call(
        message_kernel,
        out_shape=jax.ShapeDtypeStruct((MSG, HALF), BF16),
        in_specs=[VMEM, VMEM],
        out_specs=VMEM,
        cost_estimate=pl.CostEstimate(
            flops=2 * TOK * HALF * HEADS, bytes_accessed=800_000, transcendentals=0
        ),
        name="message",
    )(kv, direction)


def weights(shard, rew_ref, turn_ref, base_ref, dest_ref):
    sub, lane = iota((TOK, TOK), 0), iota((TOK, TOK), 1)
    diag = sub == lane

    def column(row):
        return jnp.sum(jnp.where(diag, row, 0.0), axis=1, keepdims=True)

    spot = iota((1, TOK), 1)
    begins = (turn_ref[...] == 1) | ((shard == 0) & (spot == 0))
    start_row = jnp.where(begins, 1.0, 0.0)
    start_col = column(start_row)
    c_row = jnp.sum(jnp.where(sub <= lane, start_col, 0.0), axis=0, keepdims=True)
    c_col = jnp.sum(jnp.where(lane <= sub, start_row, 0.0), axis=1, keepdims=True)
    rewards = column(rew_ref[...])
    base = column(base_ref[...])
    gap = c_col - c_row
    opens = start_col > 0.5
    m = jnp.where((sub > lane) & opens, (1.0 - TRACE) * jnp.exp((gap - 1.0) * LOG_TRACE), 0.0)
    decay = jnp.where(sub >= lane, jnp.exp(gap * LOG_TRACE), 0.0)
    known = jnp.sum(decay * rewards + m * base, axis=0, keepdims=True)
    total = jnp.sum(start_row, axis=1, keepdims=True)
    b_col = jnp.where(opens, (1.0 - TRACE) * jnp.exp((c_col - 1.0) * LOG_TRACE), 0.0)
    b_row = jnp.sum(jnp.where(diag, b_col, 0.0), axis=0, keepdims=True)
    b_known = jnp.sum(b_col * base + jnp.exp(c_col * LOG_TRACE) * rewards, axis=0, keepdims=True)
    dest = dest_ref[...]
    to_group = lax.rem(dest, 8).astype(F32)
    to_seq = (dest // 8).astype(F32)
    group_col = column(to_group)
    rank = jnp.sum(jnp.where((group_col == to_group) & (lane < sub), 1.0, 0.0), axis=1, keepdims=True)
    slot = (group_col * 32.0 + rank).astype(jnp.int32)
    onehot = jnp.where(slot == lane, 1.0, 0.0).astype(BF16)
    wide = (1, TOK)
    rows = [
        base_ref[...],
        known,
        jnp.exp((total - c_row) * LOG_TRACE),
        to_seq,
        jnp.broadcast_to(jnp.exp(total * LOG_TRACE), wide),
        jnp.broadcast_to(b_known, wide),
        jnp.zeros(wide, F32),
        jnp.zeros(wide, F32),
    ]
    return m, onehot, jnp.concatenate(rows, axis=0), b_row


def attend_kernel(slots, arrays, earlier, place_ref, list_ref, q_ref, *rest):
    count = len(slots)
    has_own = 0 in slots
    msgs, rest = rest[:arrays], rest[arrays:]
    if earlier:
        before_ref, *late_refs = rest[:LATE]
        val_ref, pay_ref, table, score0, score1, found, sems, out_ref = rest[LATE:]
        scores = (score0, score1)
    else:
        out_ref, table, *scores, found, sems = rest
    shard = place_ref[0]
    core = lax.rem(shard, 2)

    copies = []
    sources = [msg.at[at : at + MSG] for msg in msgs for at in range(0, msg.shape[0], MSG)]
    for i, source in enumerate(sources):
        copies.append(pltpu.make_async_copy(source, table.at[i], sems.at[i]))
    for copy in copies:
        copy.start()

    for qb in range(2):
        block = shard * 2 + qb
        n = jnp.int32(0)
        entries = [list_ref[qb, j] for j in range(LIST)]
        for j in range(LIST):
            found[qb, j] = 0
        for j in range(LIST):
            entry = entries[j]
            use = entry < block
            for i in range(j):
                use = use & (entries[i] != entry)
            back = shard - entry // 2
            even = lax.rem(back, 2) == 0
            slot = jnp.where(even, back // 2, 4 + lax.rem(back // 2 + 1 - core, 4))
            local = jnp.int32(0)
            here = jnp.bool_(False)
            for i, s in enumerate(slots):
                hit = slot == s
                local = jnp.where(hit, 2 * i, local)
                here = here | hit
            use = use & here
            at = jnp.minimum(n, LIST - 1)
            found[qb, at] = jnp.where(use, local + lax.rem(entry, 2), found[qb, at])
            n = n + jnp.where(use, 1, 0)
        found[qb, LIST] = n
    out_ref[...] = jnp.zeros_like(out_ref)
    if earlier:
        m, onehot, fields, b_row = weights(shard, *late_refs)
    for copy in copies:
        copy.wait()

    causal = iota((BLK, BLK), 1) <= iota((BLK, BLK), 0)
    lane_pair = iota((BLK, 2 * HEADS), 1)
    lane_head = iota((BLK, HEADS), 1)
    ones = jnp.ones((HEADS, BLK), BF16)

    def step(index, carry):
        qb, side = index // 2, lax.rem(index, 2)
        rows = pl.ds(pl.multiple_of(qb * BLK, BLK), BLK)
        n = found[qb, LIST]

        def run(blocks):
            codes = [qb] if has_own else []
            codes += [found[qb, j] for j in range(blocks - len(codes))]
            spots = [(code // 2, pl.multiple_of(lax.rem(code, 2) * BLK, BLK)) for code in codes]
            read = jnp.concatenate(
                [
                    jnp.concatenate(
                        [
                            table[i, TOK:MSG, pl.ds(at, BLK)],
                            table[i, TOK:MSG, pl.ds(pl.multiple_of(at + TOK, BLK), BLK)],
                        ],
                        axis=0,
                    )
                    for i, at in spots
                ],
                axis=1,
            )
            read = jnp.concatenate([read, jnp.concatenate([ones] * blocks, axis=1)], axis=0)
            for k in range(KEYS):
                first = (side * KEYS + k) * PER * HD
                heads = [q_ref[rows, pl.ds(pl.multiple_of(first + g * HD, HD), HD)] for g in range(PER)]
                query = jnp.concatenate(heads, axis=0)
                own = pl.ds(pl.multiple_of((side * KEYS + k) * HD, HD), HD)
                for j in range(0, blocks, 2):
                    both = jnp.concatenate([table[i, pl.ds(at, BLK), own] for i, at in spots[j : j + 2]], axis=0)
                    scores[k][:, j * BLK : min(j + 2, blocks) * BLK] = lax.dot_general(
                        query, both, NT, preferred_element_type=F32
                    )
            sums = jnp.zeros((BLK, 2 * HEADS), F32)
            peaks = jnp.zeros((BLK, HEADS), F32)
            for k in range(KEYS):
                for g in range(PER):
                    parts = []
                    for j in range(blocks):
                        s = scores[k][g * BLK : (g + 1) * BLK, j * BLK : (j + 1) * BLK]
                        if has_own and j == 0:
                            s = jnp.where(causal, s, LOW)
                        parts.append(s)
                    top = parts[0]
                    for s in parts[1:]:
                        top = jnp.maximum(top, s)
                    peak = jnp.max(top, axis=1, keepdims=True) * TO_LOG2
                    p = jnp.concatenate([jnp.exp2(s * TO_LOG2 - peak).astype(BF16) for s in parts], axis=1)
                    both = lax.dot_general(p, read, NT, preferred_element_type=F32)
                    head = (side * KEYS + k) * PER + g
                    sums = jnp.where((lane_pair == head) | (lane_pair == head + HEADS), both, sums)
                    peaks = jnp.where(lane_head == head, peak, peaks)
            out_ref[0, rows, 0 : 2 * HEADS] += sums
            out_ref[1, rows, 0:HEADS] += peaks

        def nothing():
            mine = lane_head // (HEADS // 2) == side
            out_ref[1, rows, 0:HEADS] += jnp.where(mine, LOW, 0.0)

        for others in range(min(LIST, 2 * count) + 1):

            @pl.when(n == others)
            def _(others=others):
                if others + has_own:
                    run(others + has_own)
                else:
                    nothing()

        return carry

    lax.fori_loop(0, 4, step, 0)

    if earlier:
        every = [out_ref, before_ref]
        peaks = [ref[1, :, 0:HEADS] for ref in every]
        top = peaks[0]
        for peak in peaks[1:]:
            top = jnp.maximum(top, peak)
        total = summed = 0.0
        for ref, peak in zip(every, peaks):
            weight = jnp.exp2(peak - top)
            total = total + ref[0, :, HEADS : 2 * HEADS] * weight
            summed = summed + ref[0, :, 0:HEADS] * weight
        att = jnp.sum(summed / total, axis=1, keepdims=True)
        diag = iota((TOK, TOK), 0) == iota((TOK, TOK), 1)
        att_row = jnp.sum(jnp.where(diag, att, 0.0), axis=0, keepdims=True)
        value = fields[0:1] + att_row
        val_ref[...] = value
        local = fields[1:2] + jnp.sum(m * att, axis=0, keepdims=True)
        b = fields[5:6] + jnp.sum(b_row * att_row, axis=1, keepdims=True)
        lines = jnp.concatenate([value, local, fields[2:5], b, fields[6:8]], axis=0)
        split = jnp.concatenate(three(lines), axis=0)
        moved = jnp.dot(split, onehot, preferred_element_type=F32)
        moved = moved[0:8] + moved[8:16] + moved[16:24]
        pay_ref[...] = jnp.zeros_like(pay_ref)
        for g in range(8):
            pay_ref[g, :, 0:32] = moved[:, g * 32 : (g + 1) * 32]


def attend(slots, place, lists, q, msgs, befores=(), extra=()):
    count = len(slots)
    partial = (2, TOK, BLK)
    most = min(LIST, 2 * count) + (0 in slots)
    scratch = [
        pltpu.VMEM((count, MSG, HALF), BF16),
        pltpu.VMEM((PER * BLK, most * BLK), F32),
        pltpu.VMEM((PER * BLK, most * BLK), F32),
        pltpu.SMEM((2, LIST + 1), jnp.int32),
        pltpu.SemaphoreType.DMA((count,)),
    ]
    late = ()
    if befores:
        out_shape = (jax.ShapeDtypeStruct((1, TOK), F32), jax.ShapeDtypeStruct((8, 8, HD), F32))
        out_specs = (VMEM, VMEM)
        late = (*befores, *extra)
        scratch.append(pltpu.VMEM(partial, F32))
    else:
        out_shape, out_specs = jax.ShapeDtypeStruct(partial, F32), VMEM
    return pl.pallas_call(
        lambda *refs: attend_kernel(slots, len(msgs), len(befores), *refs),
        out_shape=out_shape,
        in_specs=[SMEM, SMEM, VMEM] + [ANY] * len(msgs) + [VMEM] * len(late),
        out_specs=out_specs,
        scratch_shapes=scratch,
        compiler_params=pltpu.CompilerParams(vmem_limit_bytes=32 * 1024 * 1024),
        cost_estimate=pl.CostEstimate(
            flops=1_000_000, bytes_accessed=100_000, transcendentals=0
        ),
        name="attend",
    )(place, lists, q, *msgs, *late)


def sort_kernel(in_ref, out_ref):
    seqs = iota((64, HD), 0)
    lane = iota((64, HD), 1)
    before = jnp.where(iota((HD, HD), 0) < iota((HD, HD), 1), 1.0, 0.0).astype(BF16)
    ahead = jnp.zeros((64, 1), F32)
    onehots, fields = [], []
    known = jnp.zeros((1, HD), F32)
    lane_row = iota((1, HD), 1)
    zero = jnp.zeros((1, HD), F32)
    for g in range(8):
        x = in_ref[g]
        tag = x[3:4].astype(jnp.int32)
        hit = (seqs == tag) & (lane < 32)
        one = jnp.where(hit, 1.0, 0.0)
        onehot = one.astype(BF16)
        counts = jnp.dot(onehot, before, preferred_element_type=F32) + ahead
        rank = jnp.sum(one * counts, axis=0, keepdims=True)
        ahead = ahead + jnp.sum(one, axis=1, keepdims=True)
        group = jnp.full((1, HD), float(g), F32)
        rows = [
            jnp.where(rank == float(r), f, zero)
            for f in (x[0:1], x[1:2], x[2:3], group)
            for r in range(4)
        ]
        onehots.append(onehot)
        fields.append(jnp.concatenate(rows, axis=0))
        known = jnp.where(lane_row == 16 + g, x[4:5, 0:1], known)
        known = jnp.where(lane_row == 24 + g, x[5:6, 0:1], known)
    table = jnp.concatenate(fields, axis=1)
    onehot = jnp.concatenate(onehots, axis=1)
    moved = 0.0
    for part in three(table):
        moved = moved + lax.dot_general(onehot, part, NT, preferred_element_type=F32)
    moved = jnp.concatenate([moved, jnp.zeros((64, HD - 16), F32)], axis=1)
    out_ref[...] = moved + known


def sort_part(received):
    return pl.pallas_call(
        sort_kernel,
        out_shape=jax.ShapeDtypeStruct((64, HD), F32),
        in_specs=[VMEM],
        out_specs=VMEM,
        cost_estimate=pl.CostEstimate(flops=10_000_000, bytes_accessed=70_000, transcendentals=0),
        name="sort_part",
    )(received)


def finish_kernel(in_ref, adv_ref, ret_ref):
    x = in_ref[...]
    seqs = iota((64, HD), 0)
    lane = iota((64, HD), 1)
    factor = x
    offset = pltpu.roll(x, HD - 8, axis=1)
    span = 1
    while span < 64:
        inside = seqs < 64 - span
        next_factor = jnp.where(inside, pltpu.roll(factor, 64 - span, axis=0), 1.0)
        next_offset = jnp.where(inside, pltpu.roll(offset, 64 - span, axis=0), 0.0)
        offset = offset + factor * next_offset
        factor = factor * next_factor
        span *= 2
    incoming = jnp.where(seqs < 63, pltpu.roll(offset, 63, axis=0), 0.0)
    wide = (64, TOK)
    spot = iota(wide, 1) - 4 * iota(wide, 0)
    adv = jnp.zeros(wide, F32)
    ret = jnp.zeros(wide, F32)
    for r in range(4):
        group = x[:, 12 + r : 13 + r].astype(jnp.int32)
        entry = jnp.sum(jnp.where(lane == group + 16, incoming, 0.0), axis=1, keepdims=True)
        returns = x[:, 4 + r : 5 + r] + x[:, 8 + r : 9 + r] * entry
        advantage = returns - x[:, r : r + 1]
        adv = jnp.where(spot == r, advantage, adv)
        ret = jnp.where(spot == r, returns, ret)
    adv_ref[...] = jnp.sum(adv, axis=0, keepdims=True)
    ret_ref[...] = jnp.sum(ret, axis=0, keepdims=True)


def finish(arrived):
    return pl.pallas_call(
        finish_kernel,
        out_shape=(jax.ShapeDtypeStruct((1, TOK), F32),) * 2,
        in_specs=[VMEM],
        out_specs=(VMEM, VMEM),
        cost_estimate=pl.CostEstimate(flops=500_000, bytes_accessed=40_000, transcendentals=0),
        name="finish",
    )(arrived)


YS = 8


def swap(value, count):
    return lax.ppermute(value, "seq", [(s, s ^ 1) for s in range(count)])


def hop(value, chips, count):
    return lax.ppermute(value, "seq", [(s, s + 2 * chips) for s in range(count - 2 * chips)])


def place_of(x, y, core):
    return (x * YS + y) * 2 + core


def shards(queries, keys_values, block_list, value_dir, base_values, rewards, turn_start, actor_shard):
    count = lax.axis_size("seq")
    shard = lax.axis_index("seq").astype(jnp.int32)
    place = shard[None]
    core = shard % 2
    heads = (place, block_list[0], queries[0])
    own = message(keys_values[0], value_dir.reshape(HEADS, HD))
    a = hop(own, 1, count)
    b = hop(own, 2, count)
    back, last = [], []
    for s in range(count):
        x, y = s // (2 * YS), s // 2 % YS
        if s % 2 == 0:
            last.append((s, s + 1))
        elif s + 7 < count:
            between = place_of(x, (y - 2) % YS, 1)
            back.append((s, between))
            last.append((between, s + 7))
    relayed = lax.ppermute(own, "seq", back)
    sums0 = attend((0, 1), *heads, (own, a))
    sent = jnp.where(core == 0, own, relayed)
    a, b, sent, sums0 = lax.optimization_barrier((a, b, sent, sums0))
    c = hop(b, 1, count)
    far = lax.ppermute(sent, "seq", last)
    wab = swap(jnp.concatenate([a, b], axis=0), count)
    wc = swap(c, count)
    extra = (rewards, turn_start, base_values, actor_shard)
    values, payload = attend((5, 6, 2, 4, 3, 7), *heads, (wab, b, far, c, wc), (sums0,), extra)
    received = lax.all_to_all(payload, "group", split_axis=0, concat_axis=0, tiled=True)
    arranged = sort_part(received)
    arrived = lax.all_to_all(arranged, "seq", split_axis=0, concat_axis=0, tiled=True)
    advantage, returns = finish(arrived)
    return values, advantage.reshape(TOK), returns.reshape(TOK)


def solution(mesh):
    placed = (
        P("group", "seq", None),
        P("group", "seq", None),
        P("group", "seq", None),
        P(),
        P("group", "seq"),
        P("group", "seq"),
        P("group", "seq"),
        P("group", "seq"),
    )
    return jax.shard_map(
        shards,
        mesh=mesh,
        in_specs=placed,
        out_specs=(P("group", "seq"), P(("seq", "group")), P(("seq", "group"))),
        check_vma=False,
    )
```
